32 devices in a mesh: ens: 2 (over y), tile: 4 (over z), section: 2 (over x), chan: 2 (over core).
Axes of the slice: x: 2, y: 2, z: 4, core: 2. Of those that a mesh axis runs over, the one named last changes fastest.
Arguments:
- activation: bfloat16 [2, 192, 14, 14, 192], P('section', ('ens', 'tile'), None, None, 'chan'), parts along dimension 1, may hold values from -6 to 6
- boundary: bfloat16 [2, 192, 14, 14, 192], P('section', ('ens', 'tile'), None, None, 'chan'), parts along dimension 1, may hold values from -6 to 6
- conv_weight: bfloat16 [2, 5, 192, 192], P('section', None, None, 'chan'), may hold values from -0.1875 to 0.1875
- neighbours: int32 [96, 4], replicated, may hold values from 0 to 95, as said below
- rotations: int32 [96, 4], replicated, may hold values from 0 to 3, as said below
Outputs:
- input_grad: bfloat16 [2, 192, 14, 14, 192], P('section', ('ens', 'tile'), None, None, 'chan'), parts along dimension 1
- weight_grad: float32 [2, 10, 192, 192], P('section', 'ens', 'tile', 'chan'), parts along dimension 1
The draws below stay inside these ranges and needn't reach their ends.
There are 2 independent parts, one for each index of `ens`. The reference program is written for one: setup_inputs(seed, part) draws one part's arguments, and reference() takes and returns one part's arrays. A program takes and returns all parts, laid end to end along the dimension named above; an argument that names none is the same for every part. Nothing has to cross between parts.
Inputs may be any that keep to these rules, and one draw needn't show every extreme that they name: The 96 tiles are those of a cube whose faces hold equal square grids of tiles, stored in a drawn order and each turned by a drawn number of quarter turns; neighbours name the four tiles beside a tile's edges, four different ones, and every tile is named four times. `rotations`: turning tile neighbours[t, k] by this many quarter turns makes its cells continue tile t's across edge k.
All inputs are finite; a program needn't handle non-finite values.
Results may differ from the reference program's by a relative error of at most 0.003.
Values may be sent and summed in bfloat16 or wider, within the bound.
A program may use at most 128 MiB of HBM per device.

```python
import math
import jax
import jax.numpy as jnp
import numpy as np

C = 192
S = 14
TILES = 96
N_SECTION = 2


FACE_FRAMES = (((1, 0, 0), (0, 1, 0), (0, 0, 1)), ((-1, 0, 0), (0, 0, 1), (0, 1, 0)), ((0, 1, 0), (0, 0, 1), (1, 0, 0)), ((0, -1, 0), (1, 0, 0), (0, 0, 1)), ((0, 0, 1), (1, 0, 0), (0, 1, 0)), ((0, 0, -1), (0, 1, 0), (1, 0, 0)))


def frame_arrays(face_number, edge_tiles):
    normal = np.array(FACE_FRAMES[face_number][0], dtype=np.int32)
    downward = np.array(FACE_FRAMES[face_number][1], dtype=np.int32)
    rightward = np.array(FACE_FRAMES[face_number][2], dtype=np.int32)
    anchor = 2 * edge_tiles * np.maximum(normal, 0)
    return (normal, downward, rightward, anchor)


def inner_product(first, second):
    return int(np.sum(first * second))


def same_vector(first, second):
    return int(np.sum(np.abs(first - second))) == 0


def cube_tables(edge_tiles):
    per_face = edge_tiles * edge_tiles
    adjacent = np.zeros((6 * per_face, 4), np.int32)
    relative = np.zeros((6 * per_face, 4), np.int32)
    for face_number in range(6):
        normal, downward, rightward, anchor = frame_arrays(face_number, edge_tiles)
        for i in range(edge_tiles):
            for j in range(edge_tiles):
                centre = anchor + (2 * i + 1) * downward + (2 * j + 1) * rightward
                for k, stride in enumerate((-downward, -rightward, downward, rightward)):
                    stepped = centre + 2 * stride
                    down_coord = inner_product(stepped - anchor, downward)
                    right_coord = inner_product(stepped - anchor, rightward)
                    if 0 < down_coord < 2 * edge_tiles and 0 < right_coord < 2 * edge_tiles:
                        target = face_number
                        landing = stepped
                        heading = -stride
                    else:
                        target = [m for m in range(6) if same_vector(np.array(FACE_FRAMES[m][0], dtype=np.int32), stride)][0]
                        landing = centre + stride - normal
                        heading = normal
                    other_normal, other_down, other_right, other_anchor = frame_arrays(target, edge_tiles)
                    row_tile = inner_product(landing - other_anchor, other_down) // 2
                    col_tile = inner_product(landing - other_anchor, other_right) // 2
                    candidates = (-other_down, -other_right, other_down, other_right)
                    back_side = [m for m in range(4) if same_vector(candidates[m], heading)][0]
                    adjacent[face_number * per_face + i * edge_tiles + j, k] = target * per_face + row_tile * edge_tiles + col_tile
                    relative[face_number * per_face + i * edge_tiles + j, k] = (k + 2 - back_side) % 4
    return (adjacent, relative)


def tiling(key):
    edge_tiles = math.isqrt(TILES // 6)
    adjacent, relative = cube_tables(edge_tiles)
    placement = jax.random.permutation(jax.random.fold_in(key, 101), TILES)
    quarter = jax.random.randint(jax.random.fold_in(key, 202), (TILES,), 0, 4)
    position = jnp.argsort(placement)
    geometric = placement[:, None]
    geo_side = (jnp.arange(4)[None, :] - quarter[geometric]) % 4
    neighbour_geo = jnp.asarray(adjacent)[geometric, geo_side]
    turn_geo = jnp.asarray(relative)[geometric, geo_side]
    stored_turn = (turn_geo - quarter[neighbour_geo] + quarter[geometric]) % 4
    return (position[neighbour_geo].astype(jnp.int32), stored_turn.astype(jnp.int32))


def draw_neighbours(key, part):
    return tiling(key)[0]


def draw_rotations(key, part):
    return tiling(key)[1]


def block_levels(own_key, extent, cuts, least, largest):
    loudness, own = 1.0, jax.random.fold_in(own_key, 6)
    for dim, shards_of in cuts:
        heights = jnp.exp(jax.random.uniform(jax.random.fold_in(own, dim), (shards_of,), jnp.float32, least / len(cuts), largest / len(cuts)))
        loudness = loudness * jnp.repeat(heights, extent[dim] // shards_of).reshape([-1 if axis == dim else 1 for axis in range(len(extent))])
    return loudness


def centred(rng, dims, scale, limit, shards=(), kind=jnp.bfloat16):
    gain = block_levels(rng, dims, shards, -0.22, 0.18) if shards else 1.0
    values = jax.random.normal(rng, dims, jnp.float32) * scale * gain
    return jnp.minimum(jnp.maximum(values, -limit), limit).astype(kind)


def setup_inputs(seed: int = 0, part: int = 0) -> dict:
    splits = jax.random.split(jax.random.key(seed), 6)
    part_keys = jax.random.split(jax.random.fold_in(splits[5], part), 6)
    return {
        "activation": centred(part_keys[0], (N_SECTION, TILES, S, S, C), 1.0, 6.0, ((0, 2), (1, 4), (4, 2))),
        "boundary": centred(part_keys[1], (N_SECTION, TILES, S, S, C), 1.0, 6.0, ((0, 2), (1, 4), (4, 2))),
        "conv_weight": centred(splits[2], (N_SECTION, 5, C, C), (5 * C) ** -0.5, 0.1875, ((0, 2), (3, 2))),
        "neighbours": draw_neighbours(jax.random.fold_in(splits[5], 71), part),
        "rotations": draw_rotations(jax.random.fold_in(splits[5], 71), part),
    }


TAP_OFFSETS = ((0, 0), (-1, 0), (0, -1), (1, 0), (0, 1))


def edges_of(field):
    return jnp.stack([field[:, 0], field[:, :, 0], field[:, -1], field[:, :, -1]], axis=1)


def padded_field(field, neighbours, rotations):
    edge_table = jnp.stack([edges_of(jnp.rot90(field, turn_count, axes=(1, 2))) for turn_count in range(4)])
    opposite = (jnp.arange(4, dtype=jnp.int32)[None, :] + 2) % 4
    strips = edge_table[rotations, neighbours, opposite]
    padded = jnp.pad(field, ((0, 0), (1, 1), (1, 1), (0, 0)))
    padded = padded.at[:, 0, 1:-1].set(strips[:, 0])
    padded = padded.at[:, 1:-1, 0].set(strips[:, 1])
    padded = padded.at[:, -1, 1:-1].set(strips[:, 2])
    padded = padded.at[:, 1:-1, -1].set(strips[:, 3])
    return padded


def shifted_view(padded, offset, tile_side):
    row_shift, col_shift = offset
    return padded[:, 1 - row_shift:1 - row_shift + tile_side, 1 - col_shift:1 - col_shift + tile_side]


def reference(activation, boundary, conv_weight, neighbours, rotations):
    incoming = jnp.roll(boundary, -1, axis=0)
    normalizer = float(TILES * S * S) ** -0.5
    input_parts = []
    weight_parts = []
    for section_index in range(N_SECTION):
        saved_input = activation[section_index].astype(jnp.float32)
        logistic = jax.nn.sigmoid(saved_input)
        activated = (saved_input * logistic).astype(jnp.bfloat16)
        grad_pad = padded_field(incoming[section_index], neighbours, rotations)
        weights = conv_weight[section_index].astype(jnp.float32)
        act_grad = jnp.zeros(saved_input.shape, jnp.float32)
        tap_grads = []
        for tap_index in range(5):
            tap_view = shifted_view(grad_pad, TAP_OFFSETS[tap_index], S).astype(jnp.float32)
            act_grad = act_grad + jnp.einsum("tijo,co->tijc", tap_view, weights[tap_index])
            tap_grads.append(jnp.einsum("tijc,tijo->co", activated.astype(jnp.float32), tap_view))
        derivative = logistic * (1.0 + saved_input * (1.0 - logistic))
        input_parts.append((derivative * act_grad).astype(jnp.bfloat16))
        weight_parts.append(jnp.stack(tap_grads) * normalizer)
    return jnp.stack(input_parts), jnp.stack(weight_parts)
```

```python
import functools

import jax
import jax.numpy as jnp
from jax import lax
from jax.experimental import pallas as pl
from jax.experimental.pallas import tpu as pltpu
from jax.sharding import PartitionSpec as P

MESH = pl.DeviceIdType.MESH
LANES = 128
F32 = jnp.float32
BF16 = jnp.bfloat16


def flat(x):
    return x.reshape(-1, x.shape[-1])


def kernel(
    n_tile, n_section, normalizer,
    act_ref, bnd_ref, w_ref, idx_ref,
    grad_ref, wg_ref,
    peri_src, inner_src, ring, inner, third, pad, wother, wfull, activ, deriv, acc, wsend, wrecv,
    x_send, x_recv, z_send, z_recv, w_sems, c_send, c_recv, h_send, h_recv, g_send, g_recv,
):
    ens, me, sec, chan = (lax.axis_index(a) for a in ("ens", "tile", "section", "chan"))
    side, _, tiles, ch = act_ref.shape
    full = side - 1
    half_tiles = n_tile // 2
    other = 1 - chan
    sibling = (ens, me, sec, other)
    target = (ens, me, lax.rem(sec + n_section - 1, n_section), chan)
    source = (ens, me, lax.rem(sec + 1, n_section), chan)
    lead = ch // 3

    def remote(src, dst, ss, rs, dev):
        return pltpu.make_async_remote_copy(
            src_ref=src, dst_ref=dst, send_sem=ss, recv_sem=rs, device_id=dev, device_id_type=MESH
        )

    barrier = pltpu.get_barrier_semaphore()
    for dev in (sibling, target, source):
        pl.semaphore_signal(barrier, inc=1, device_id=dev, device_id_type=MESH)
    for step in range(1, n_tile):
        for k in range(2):
            dev = (ens, lax.rem(me + step, n_tile), sec, k)
            pl.semaphore_signal(barrier, inc=1, device_id=dev, device_id_type=MESH)

    rows_i = lax.broadcasted_iota(jnp.int32, (ch, LANES), 0)
    cols_i = lax.broadcasted_iota(jnp.int32, (ch, LANES), 1)
    eye = (rows_i == cols_i).astype(BF16)
    picks = [
        ((cols_i >= ch) & (rows_i - b * lead == cols_i - ch)).astype(BF16) for b in range(3)
    ]

    def pack(groups, store):
        tail = groups[3]
        for b in range(3):
            out = jnp.dot(groups[b], eye, preferred_element_type=F32) + jnp.dot(
                tail, picks[b], preferred_element_type=F32
            )
            store(b, out.astype(BF16).reshape(-1, tiles, LANES))

    wide_i = lax.broadcasted_iota(jnp.int32, (LANES, LANES), 0)
    wide_j = lax.broadcasted_iota(jnp.int32, (LANES, LANES), 1)
    moves = [
        ((wide_i >= ch) & (wide_j == wide_i - ch + b * lead)).astype(BF16) for b in range(3)
    ]

    def untail(blocks):
        total = jnp.dot(blocks[0], moves[0], preferred_element_type=F32)
        for b in range(1, 3):
            total = total + jnp.dot(blocks[b], moves[b], preferred_element_type=F32)
        return total.astype(BF16)

    def keep(x):
        lane = lax.broadcasted_iota(jnp.int32, x.shape, x.ndim - 1)
        return jnp.where(lane < ch, x.astype(F32), 0.0).astype(BF16)

    def put_peri(b, x):
        peri_src[b] = x

    pack(
        [
            flat(bnd_ref[0, 0:full]),
            flat(bnd_ref[0:full, full]),
            flat(bnd_ref[full, 1 : full + 1]),
            flat(bnd_ref[1 : full + 1, 0]),
        ],
        put_peri,
    )
    pl.semaphore_wait(barrier, 3 + 2 * (n_tile - 1))
    send_peri = remote(peri_src, ring.at[me], x_send.at[0], x_recv.at[0], target)
    send_peri.start()
    mine_c = pl.multiple_of(chan * ch, 16)
    other_c = pl.multiple_of(other * ch, 16)
    send_w = remote(w_ref.at[:, pl.ds(other_c, ch), :], wother, w_sems.at[0], w_sems.at[1], sibling)
    send_w.start()
    n_chunk = inner.shape[0]
    sends_inner = []
    for m in range(n_chunk):
        first = 1 + 4 * m

        def put_inner(b, x, m=m):
            inner_src[m, b] = x

        pack([flat(bnd_ref[first + g, 1:full]) for g in range(4)], put_inner)
        copy = remote(
            inner_src.at[m], inner.at[m], x_send.at[1 + m], x_recv.at[1 + m], target
        )
        copy.start()
        sends_inner.append(copy)

    acc[...] = jnp.zeros_like(acc)

    def silu_row(i, carry):
        v = act_ref[i].astype(F32)
        logistic = 1.0 / (1.0 + jnp.exp(-v))
        activ[i] = (v * logistic).astype(BF16)
        deriv[i] = logistic * (1.0 + v * (1.0 - logistic))
        return carry

    lax.fori_loop(0, side, silu_row, 0)
    wfull[...] = jnp.zeros_like(wfull)
    wfull[:, :, 0:ch] = w_ref[:, pl.ds(mine_c, ch), :]
    send_w.wait()
    wfull[:, :, LANES : LANES + ch] = wother[...]

    send_peri.wait()
    sends_z = []
    for step in range(1, n_tile):
        dev = (ens, lax.rem(me + step, n_tile), sec, chan)
        copy = remote(ring.at[me], ring.at[me], z_send.at[step - 1], z_recv.at[step - 1], dev)
        copy.start()
        sends_z.append(copy)
    blocks = [ring[me, b] for b in range(3)]
    tail = untail([flat(x) for x in blocks]).reshape(-1, tiles, LANES)
    pad[1, 1 : full + 1, :, 0:LANES] = keep(blocks[0])
    pad[1 : full + 1, full + 1, :, 0:LANES] = keep(blocks[1])
    pad[full + 1, 2 : full + 2, :, 0:LANES] = keep(blocks[2])
    pad[2 : full + 2, 1, :, 0:LANES] = tail

    def to_sibling(rows, cols, ss, rs):
        return remote(
            pad.at[rows, cols, :, 0:LANES], pad.at[rows, cols, :, LANES : 2 * LANES], ss, rs, sibling
        )

    inside = pl.ds(1, side)
    sends_c = [
        to_sibling(pl.ds(1, 1), inside, c_send.at[n_chunk], c_recv.at[n_chunk]),
        to_sibling(pl.ds(side, 1), inside, c_send.at[n_chunk + 1], c_recv.at[n_chunk + 1]),
    ]
    for copy in sends_c:
        copy.start()
    for m in range(n_chunk):
        sends_inner[m].wait()
        first = 2 + 4 * m
        blocks = [inner[m, b] for b in range(3)]
        for b in range(3):
            pad[first + b, 2 : full + 1, :, 0:LANES] = keep(blocks[b])
        pad[first + 3, 2 : full + 1, :, 0:LANES] = untail([flat(x) for x in blocks]).reshape(
            -1, tiles, LANES
        )
        copy = to_sibling(pl.ds(first, 4), inside, c_send.at[m], c_recv.at[m])
        copy.start()
        sends_c.append(copy)

    for copy in sends_z:
        copy.wait()
    for z in range(n_tile):
        third[z] = untail([flat(ring[z, b]) for b in range(3)]).reshape(-1, tiles, LANES)

    def edge(s, p):
        if s == 0:
            part = ring[:, 0, p] if p < full else ring[:, 1, 0]
        elif s == 3:
            part = ring[:, 1, p] if p < full else ring[:, 2, full - 1]
        elif s == 2:
            part = third[:, full - 1] if p == 0 else ring[:, 2, p - 1]
        else:
            part = ring[:, 0, 0] if p == 0 else third[:, p - 1]
        return flat(part)

    n_all = n_tile * tiles
    which = idx_ref[...]
    spots = lax.broadcasted_iota(jnp.int32, (4 * tiles, 4 * n_all), 1)
    plain = (which == spots).astype(F32).astype(BF16)
    turned = (which == spots + 4 * n_all).astype(F32).astype(BF16)
    for p in range(side):
        ahead = jnp.concatenate([edge(s, p) for s in range(4)], axis=0)
        behind = jnp.concatenate([edge(s, full - p) for s in range(4)], axis=0)
        strip = jnp.dot(plain, ahead, preferred_element_type=F32) + jnp.dot(
            turned, behind, preferred_element_type=F32
        )
        strip = keep(strip).reshape(4, tiles, LANES)
        pad[0, 1 + p, :, 0:LANES] = strip[0]
        pad[1 + p, 0, :, 0:LANES] = strip[1]
        pad[side + 1, 1 + p, :, 0:LANES] = strip[2]
        pad[1 + p, side + 1, :, 0:LANES] = strip[3]
    sends_h = [
        to_sibling(rows, cols, h_send.at[n], h_recv.at[n])
        for n, (rows, cols) in enumerate(
            (
                (pl.ds(0, 1), inside),
                (inside, pl.ds(0, 1)),
                (pl.ds(side + 1, 1), inside),
                (inside, pl.ds(side + 1, 1)),
            )
        )
    ]
    for copy in sends_h:
        copy.start()
    for copy in sends_c + sends_h:
        copy.wait()

    def row(i, carry):
        a = flat(activ[i])
        total = None
        for q, (di, dj) in enumerate(((0, 0), (-1, 0), (0, -1), (1, 0), (0, 1))):
            view = flat(pad[i + 1 - di, 1 - dj : 1 - dj + side])
            term = lax.dot_general(
                view, wfull[q], (((1,), (1,)), ((), ())), preferred_element_type=F32
            )
            total = term if total is None else total + term
            acc[q] += lax.dot_general(
                a, view, (((0,), (0,)), ((), ())), preferred_element_type=F32
            )
        grad_ref[i] = (deriv[i] * total.reshape(side, tiles, ch)).astype(BF16)
        return carry

    lax.fori_loop(0, side, row, 0)

    depth = wg_ref.shape[1]
    for j in range(half_tiles):
        for k in range(2):
            part = acc[:, j * depth : (j + 1) * depth, k * LANES : (k + 1) * LANES]
            wsend[j, k] = part.astype(wsend.dtype)
    owner = chan * half_tiles
    for j in range(half_tiles):
        for k in range(2):
            there = (ens, owner + j, sec, chan if k == 0 else other)
            copy = remote(wsend.at[j, k], wrecv.at[me], g_send.at[j, k], g_recv.at[me], there)
            if k == 0:

                @pl.when(owner + j != me)
                def _():
                    copy.start()

                @pl.when(owner + j == me)
                def _():
                    wrecv[me] = wsend[j, 0]
            else:
                copy.start()
    from_chan = me // half_tiles
    for z in range(n_tile):

        @pl.when((me != z) | (from_chan != chan))
        def _():
            remote(wsend.at[0, 0], wrecv.at[z], g_send.at[0, 0], g_recv.at[z], sibling).wait_recv()

    total = wrecv[0].astype(F32)
    for z in range(1, n_tile):
        total = total + wrecv[z].astype(F32)
    wg_ref[...] = total[:, :, 0:ch] * normalizer
    for j in range(half_tiles):
        for k in range(2):
            copy = remote(wsend.at[j, k], wrecv.at[me], g_send.at[j, k], g_recv.at[me], sibling)
            if k == 0:

                @pl.when(owner + j != me)
                def _():
                    copy.wait_send()
            else:
                copy.wait_send()


def body(n_tile, n_section, activation, boundary, conv_weight, neighbours, rotations):
    _, tiles, side, _, ch = activation.shape
    taps, c_all = conv_weight.shape[1:3]
    depth = c_all // n_tile
    n_all = n_tile * tiles
    act = jnp.transpose(activation[0], (1, 2, 0, 3))
    bnd = jnp.transpose(boundary[0], (1, 2, 0, 3))
    start = lax.axis_index("tile") * tiles
    near = lax.dynamic_slice_in_dim(neighbours.T, start, tiles, 1)
    turns = lax.dynamic_slice_in_dim(rotations.T, start, tiles, 1)
    src = (jnp.arange(4, dtype=jnp.int32)[:, None] + 2 - turns) % 4
    flipped = (turns == 2) | ((turns == 1) & (src % 2 == 0)) | ((turns == 3) & (src % 2 == 1))
    idx = (src * n_all + near + jnp.where(flipped, 4 * n_all, 0)).reshape(4 * tiles, 1)
    full = side - 1
    chunks = (side - 2) // 4
    vm = pl.BlockSpec(memory_space=pltpu.VMEM)
    normalizer = float(n_all * side * side) ** -0.5
    dma = pltpu.SemaphoreType.DMA
    grad, wg = pl.pallas_call(
        functools.partial(kernel, n_tile, n_section, normalizer),
        out_shape=(
            jax.ShapeDtypeStruct((side, side, tiles, ch), BF16),
            jax.ShapeDtypeStruct((taps, depth, ch), F32),
        ),
        in_specs=[vm] * 4,
        out_specs=(vm, vm),
        scratch_shapes=[
            pltpu.VMEM((3, full, tiles, LANES), BF16),
            pltpu.VMEM((chunks, 3, side - 2, tiles, LANES), BF16),
            pltpu.VMEM((n_tile, 3, full, tiles, LANES), BF16),
            pltpu.VMEM((chunks, 3, side - 2, tiles, LANES), BF16),
            pltpu.VMEM((n_tile, full, tiles, LANES), BF16),
            pltpu.VMEM((side + 2, side + 2, tiles, 2 * LANES), BF16),
            pltpu.VMEM((taps, ch, ch), BF16),
            pltpu.VMEM((taps, ch, 2 * LANES), BF16),
            pltpu.VMEM((side, side, tiles, ch), BF16),
            pltpu.VMEM((side, side, tiles, ch), F32),
            pltpu.VMEM((taps, ch, 2 * LANES), F32),
            pltpu.VMEM((n_tile // 2, 2, taps, depth, LANES), F32),
            pltpu.VMEM((n_tile, taps, depth, LANES), F32),
            dma((1 + chunks,)),
            dma((1 + chunks,)),
            dma((n_tile - 1,)),
            dma((n_tile - 1,)),
            dma((2,)),
            dma((chunks + 2,)),
            dma((chunks + 2,)),
            dma((4,)),
            dma((4,)),
            dma((n_tile // 2, 2)),
            dma((n_tile,)),
        ],
        compiler_params=pltpu.CompilerParams(
            collective_id=0, has_side_effects=True, vmem_limit_bytes=48 * 1024 * 1024
        ),
        cost_estimate=pl.CostEstimate(
            flops=4 * taps * side * side * tiles * ch * 2 * ch,
            bytes_accessed=3 * side * side * tiles * LANES * 2,
            transcendentals=side * side * tiles * ch,
        ),
    )(act, bnd, conv_weight[0], idx)
    return jnp.transpose(grad, (2, 0, 1, 3))[None], wg[None]


def solution(mesh):
    spec = P("section", ("ens", "tile"), None, None, "chan")
    return jax.shard_map(
        functools.partial(body, mesh.shape["tile"], mesh.shape["section"]),
        mesh=mesh,
        in_specs=(spec, spec, P("section", None, None, "chan"), P(), P()),
        out_specs=(spec, P("section", "ens", "tile", "chan")),
        check_vma=False,
    )
```

```python
import functools

import jax
import jax.numpy as jnp
from jax import lax
from jax.experimental import pallas as pl
from jax.experimental.pallas import tpu as pltpu
from jax.sharding import PartitionSpec as P

MESH = pl.DeviceIdType.MESH
LANES = 128
F32 = jnp.float32
BF16 = jnp.bfloat16
WIRE = jnp.float32


def flat(x):
    return x.reshape(-1, x.shape[-1])


def kernel(
    n_tile, n_section, normalizer,
    act_hbm, bnd_hbm, w_hbm, idx_ref,
    grad_ref, wg_ref,
    act_ref, bnd_ref, w_ref,
    peri_src, inner_src, ring, inner, third, pad, strips, wother, wfull, activ, deriv, totals, acc, wsend, wrecv,
    l_sem, x_send, x_recv, z_send, z_recv, w_sems, c_send, c_recv, h_send, h_recv, g_send, g_recv,
):
    ens, me, sec, chan = (lax.axis_index(a) for a in ("ens", "tile", "section", "chan"))
    side, _, tiles, ch = act_ref.shape
    full = side - 1
    half_tiles = n_tile // 2
    other = 1 - chan
    sibling = (ens, me, sec, other)
    target = (ens, me, lax.rem(sec + n_section - 1, n_section), chan)
    source = (ens, me, lax.rem(sec + 1, n_section), chan)
    lead = ch // 3
    n_chunk = inner.shape[0]

    def remote(src, dst, ss, rs, dev):
        return pltpu.make_async_remote_copy(
            src_ref=src, dst_ref=dst, send_sem=ss, recv_sem=rs, device_id=dev, device_id_type=MESH
        )

    loads = [
        pltpu.make_async_copy(src, dst, l_sem.at[n])
        for n, (src, dst) in enumerate(((bnd_hbm, bnd_ref), (w_hbm, w_ref), (act_hbm, act_ref)))
    ]
    for copy in loads:
        copy.start()
    barrier = pltpu.get_barrier_semaphore()
    for dev in (sibling, target, source):
        pl.semaphore_signal(barrier, inc=1, device_id=dev, device_id_type=MESH)
    for step in range(1, n_tile):
        for k in range(2):
            dev = (ens, lax.rem(me + step, n_tile), sec, k)
            pl.semaphore_signal(barrier, inc=1, device_id=dev, device_id_type=MESH)

    rows_i = lax.broadcasted_iota(jnp.int32, (ch, LANES), 0)
    cols_i = lax.broadcasted_iota(jnp.int32, (ch, LANES), 1)
    eye = (rows_i == cols_i).astype(BF16)
    picks = [
        ((cols_i >= ch) & (rows_i - b * lead == cols_i - ch)).astype(BF16) for b in range(3)
    ]
    wide_i = lax.broadcasted_iota(jnp.int32, (LANES, LANES), 0)
    wide_j = lax.broadcasted_iota(jnp.int32, (LANES, LANES), 1)
    moves = [
        ((wide_i >= ch) & (wide_j == wide_i - ch + b * lead)).astype(BF16) for b in range(3)
    ]

    def packed(groups, b):
        out = jnp.dot(groups[b], eye, preferred_element_type=F32) + jnp.dot(
            groups[3], picks[b], preferred_element_type=F32
        )
        return out.astype(BF16).reshape(-1, tiles, LANES)

    def untail(blocks):
        total = jnp.dot(blocks[0], moves[0], preferred_element_type=F32)
        for b in range(1, 3):
            total = total + jnp.dot(blocks[b], moves[b], preferred_element_type=F32)
        return total.astype(BF16).reshape(-1, tiles, LANES)

    def keep(x):
        lane = lax.broadcasted_iota(jnp.int32, x.shape, x.ndim - 1)
        return jnp.where(lane < ch, x.astype(F32), 0.0).astype(BF16)

    loads[0].wait()
    groups = [
        flat(bnd_ref[0, 0:full]),
        flat(bnd_ref[0:full, full]),
        flat(bnd_ref[full, 1 : full + 1]),
        flat(bnd_ref[1 : full + 1, 0]),
    ]
    sends_peri = []
    for b in range(3):
        peri_src[b] = packed(groups, b)
        if b == 0:
            pl.semaphore_wait(barrier, 3 + 2 * (n_tile - 1))
        copy = remote(peri_src.at[b], ring.at[me, b], x_send.at[b], x_recv.at[b], target)
        copy.start()
        sends_peri.append(copy)
    loads[1].wait()
    mine_c = pl.multiple_of(chan * ch, 16)
    other_c = pl.multiple_of(other * ch, 16)
    send_w = remote(w_ref.at[:, pl.ds(other_c, ch), :], wother, w_sems.at[0], w_sems.at[1], sibling)
    send_w.start()
    sends_inner = []
    for m in range(n_chunk):
        first = 1 + 4 * m
        groups = [flat(bnd_ref[first + g, 1:full]) for g in range(4)]
        for b in range(3):
            inner_src[m, b] = packed(groups, b)
        sends_inner.append(
            remote(inner_src.at[m], inner.at[m], x_send.at[3 + m], x_recv.at[3 + m], target)
        )
    sends_z = []
    for b in range(3):
        sends_peri[b].wait()
        if b == 0:
            sends_inner[0].start()
        for step in range(1, n_tile):
            dev = (ens, lax.rem(me + step, n_tile), sec, chan)
            copy = remote(
                ring.at[me, b], ring.at[me, b], z_send.at[step - 1, b], z_recv.at[step - 1, b], dev
            )
            copy.start()
            sends_z.append(copy)
    sends_inner[1].start()

    blocks = [ring[me, b] for b in range(3)]
    pad[1, 1 : full + 1, :, 0:LANES] = keep(blocks[0])
    pad[1 : full + 1, full + 1, :, 0:LANES] = keep(blocks[1])
    pad[full + 1, 2 : full + 2, :, 0:LANES] = keep(blocks[2])
    pad[2 : full + 2, 1, :, 0:LANES] = untail([flat(x) for x in blocks])

    def to_sibling(rows, cols, ss, rs):
        return remote(
            pad.at[rows, cols, :, 0:LANES], pad.at[rows, cols, :, LANES : 2 * LANES], ss, rs, sibling
        )

    inside = pl.ds(1, side)
    sends_c = [
        to_sibling(pl.ds(first, 1), inside, c_send.at[n_chunk + n], c_recv.at[n_chunk + n])
        for n, first in enumerate((1, side))
    ]
    for copy in sends_c:
        copy.start()

    none = jnp.zeros((side, tiles, 2 * LANES), BF16)
    pad[0, 1 : side + 1] = none
    pad[side + 1, 1 : side + 1] = none
    pad[1 : side + 1, 0] = none
    pad[1 : side + 1, side + 1] = none
    acc[...] = jnp.zeros_like(acc)
    wfull[...] = jnp.zeros_like(wfull)
    wfull[:, :, 0:ch] = w_ref[:, pl.ds(mine_c, ch), :]
    send_w.wait()
    wfull[:, :, LANES : LANES + ch] = wother[...]

    loads[2].wait()

    def silu_row(i, carry):
        v = act_ref[i].astype(F32)
        logistic = 1.0 / (1.0 + jnp.exp(-v))
        activ[i] = (v * logistic).astype(BF16)
        deriv[i] = logistic * (1.0 + v * (1.0 - logistic))
        return carry

    lax.fori_loop(0, side, silu_row, 0)

    def times(view, q):
        return lax.dot_general(
            view, wfull[q], (((1,), (1,)), ((), ())), preferred_element_type=F32
        )

    def against(a, view):
        return lax.dot_general(a, view, (((0,), (0,)), ((), ())), preferred_element_type=F32)

    def row(i, carry):
        a = flat(activ[i])
        total = None
        for q, (di, dj) in enumerate(((0, 0), (-1, 0), (0, -1), (1, 0), (0, 1))):
            view = flat(pad[i + 1 - di, 1 - dj : 1 - dj + side])
            term = times(view, q)
            total = term if total is None else total + term
            acc[q] += against(a, view)
        total = total.reshape(side, tiles, ch)
        totals[i] = total
        grad_ref[i] = (deriv[i] * total).astype(BF16)
        return carry

    for m in range(n_chunk):
        sends_inner[m].wait()
        if m + 2 < n_chunk:
            sends_inner[m + 2].start()
        first = 2 + 4 * m
        blocks = [inner[m, b] for b in range(3)]
        for b in range(3):
            pad[first + b, 2 : full + 1, :, 0:LANES] = keep(blocks[b])
        pad[first + 3, 2 : full + 1, :, 0:LANES] = untail([flat(x) for x in blocks])
        copy = to_sibling(pl.ds(first, 4), inside, c_send.at[m], c_recv.at[m])
        copy.start()
        if m == 0:
            for early in sends_c:
                early.wait()
        copy.wait()
        lax.fori_loop(4 * m, 4 * m + 4 if m + 1 < n_chunk else side, row, 0)

    depth = wg_ref.shape[1]
    owner = chan * half_tiles

    def share(part, q0, q1):
        for j in range(half_tiles):
            for k in range(2):
                wsend[j, k, q0:q1] = acc[
                    q0:q1, j * depth : (j + 1) * depth, k * LANES : (k + 1) * LANES
                ].astype(wsend.dtype)
                copy = outgoing(part, q0, q1, j, k)
                if k == 0:

                    @pl.when(owner + j != me)
                    def _():
                        copy.start()

                    @pl.when(owner + j == me)
                    def _():
                        wrecv[me, q0:q1] = wsend[j, 0, q0:q1]
                else:
                    copy.start()

    def outgoing(part, q0, q1, j, k):
        there = (ens, owner + j, sec, chan if k == 0 else other)
        return remote(
            wsend.at[j, k, q0:q1], wrecv.at[me, q0:q1], g_send.at[part, j, k], g_recv.at[part, me], there
        )

    n_tap = acc.shape[0]
    parts = ((0, 1), (1, n_tap))
    share(0, *parts[0])

    for copy in sends_z:
        copy.wait()
    for z in range(n_tile):
        third[z] = untail([flat(ring[z, b]) for b in range(3)])

    def edge(s, p):
        if s == 0:
            part = ring[:, 0, p] if p < full else ring[:, 1, 0]
        elif s == 3:
            part = ring[:, 1, p] if p < full else ring[:, 2, full - 1]
        elif s == 2:
            part = third[:, full - 1] if p == 0 else ring[:, 2, p - 1]
        else:
            part = ring[:, 0, 0] if p == 0 else third[:, p - 1]
        return flat(part)

    n_all = n_tile * tiles
    which = idx_ref[...]
    spots = lax.broadcasted_iota(jnp.int32, (4 * tiles, 4 * n_all), 1)
    plain = (which == spots).astype(F32).astype(BF16)
    turned = (which == spots + 4 * n_all).astype(F32).astype(BF16)
    for p in range(side):
        ahead = jnp.concatenate([edge(s, p) for s in range(4)], axis=0)
        behind = jnp.concatenate([edge(s, full - p) for s in range(4)], axis=0)
        strip = jnp.dot(plain, ahead, preferred_element_type=F32) + jnp.dot(
            turned, behind, preferred_element_type=F32
        )
        strips[:, p, :, 0:LANES] = keep(strip).reshape(4, tiles, LANES)
    send_h = remote(
        strips.at[:, :, :, 0:LANES], strips.at[:, :, :, LANES : 2 * LANES], h_send.at[0], h_recv.at[0], sibling
    )
    send_h.start()
    send_h.wait()
    taps_of = (3, 4, 1, 2)
    for k, q in enumerate(taps_of):
        a = (activ[0], activ[:, 0], activ[full], activ[:, full])[k]
        acc[q] += against(flat(a), flat(strips[k]))
    share(1, *parts[1])
    for k, q in enumerate(taps_of):
        term = times(flat(strips[k]), q).reshape(side, tiles, ch)
        if k == 0:
            totals[0] += term
        elif k == 1:
            totals[:, 0] += term
        elif k == 2:
            totals[full] += term
        else:
            totals[:, full] += term
    grad_ref[0] = (deriv[0] * totals[0]).astype(BF16)
    grad_ref[full] = (deriv[full] * totals[full]).astype(BF16)
    grad_ref[1:full, 0] = (deriv[1:full, 0] * totals[1:full, 0]).astype(BF16)
    grad_ref[1:full, full] = (deriv[1:full, full] * totals[1:full, full]).astype(BF16)

    from_chan = me // half_tiles
    for part, (q0, q1) in enumerate(parts):
        for z in range(n_tile):

            @pl.when((me != z) | (from_chan != chan))
            def _():
                remote(
                    wsend.at[0, 0, q0:q1], wrecv.at[z, q0:q1], g_send.at[part, 0, 0], g_recv.at[part, z], sibling
                ).wait_recv()

    total = wrecv[0].astype(F32)
    for z in range(1, n_tile):
        total = total + wrecv[z].astype(F32)
    wg_ref[...] = total[:, :, 0:ch] * normalizer
    for part, (q0, q1) in enumerate(parts):
        for j in range(half_tiles):
            for k in range(2):
                copy = outgoing(part, q0, q1, j, k)
                if k == 0:

                    @pl.when(owner + j != me)
                    def _():
                        copy.wait_send()
                else:
                    copy.wait_send()


def body(n_tile, n_section, activation, boundary, conv_weight, neighbours, rotations):
    _, tiles, side, _, ch = activation.shape
    taps, c_all = conv_weight.shape[1:3]
    depth = c_all // n_tile
    n_all = n_tile * tiles
    act = jnp.transpose(activation[0], (1, 2, 0, 3))
    bnd = jnp.transpose(boundary[0], (1, 2, 0, 3))
    start = lax.axis_index("tile") * tiles
    near = lax.dynamic_slice_in_dim(neighbours.T, start, tiles, 1)
    turns = lax.dynamic_slice_in_dim(rotations.T, start, tiles, 1)
    src = (jnp.arange(4, dtype=jnp.int32)[:, None] + 2 - turns) % 4
    flipped = (turns == 2) | ((turns == 1) & (src % 2 == 0)) | ((turns == 3) & (src % 2 == 1))
    idx = (src * n_all + near + jnp.where(flipped, 4 * n_all, 0)).reshape(4 * tiles, 1)
    full = side - 1
    chunks = (side - 2) // 4
    vm = pl.BlockSpec(memory_space=pltpu.VMEM)
    normalizer = float(n_all * side * side) ** -0.5
    dma = pltpu.SemaphoreType.DMA
    grad, wg = pl.pallas_call(
        functools.partial(kernel, n_tile, n_section, normalizer),
        out_shape=(
            jax.ShapeDtypeStruct((side, side, tiles, ch), BF16),
            jax.ShapeDtypeStruct((taps, depth, ch), F32),
        ),
        in_specs=[pl.BlockSpec(memory_space=pl.ANY)] * 3 + [vm],
        out_specs=(vm, vm),
        scratch_shapes=[
            pltpu.VMEM((side, side, tiles, ch), BF16),
            pltpu.VMEM((side, side, tiles, ch), BF16),
            pltpu.VMEM((taps, c_all, ch), BF16),
            pltpu.VMEM((3, full, tiles, LANES), BF16),
            pltpu.VMEM((chunks, 3, side - 2, tiles, LANES), BF16),
            pltpu.VMEM((n_tile, 3, full, tiles, LANES), BF16),
            pltpu.VMEM((chunks, 3, side - 2, tiles, LANES), BF16),
            pltpu.VMEM((n_tile, full, tiles, LANES), BF16),
            pltpu.VMEM((side + 2, side + 2, tiles, 2 * LANES), BF16),
            pltpu.VMEM((4, side, tiles, 2 * LANES), BF16),
            pltpu.VMEM((taps, ch, ch), BF16),
            pltpu.VMEM((taps, ch, 2 * LANES), BF16),
            pltpu.VMEM((side, side, tiles, ch), BF16),
            pltpu.VMEM((side, side, tiles, ch), F32),
            pltpu.VMEM((side, side, tiles, ch), F32),
            pltpu.VMEM((taps, ch, 2 * LANES), F32),
            pltpu.VMEM((n_tile // 2, 2, taps, depth, LANES), WIRE),
            pltpu.VMEM((n_tile, taps, depth, LANES), WIRE),
            dma((3,)),
            dma((3 + chunks,)),
            dma((3 + chunks,)),
            dma((n_tile - 1, 3)),
            dma((n_tile - 1, 3)),
            dma((2,)),
            dma((chunks + 2,)),
            dma((chunks + 2,)),
            dma((1,)),
            dma((1,)),
            dma((2, n_tile // 2, 2)),
            dma((2, n_tile)),
        ],
        compiler_params=pltpu.CompilerParams(
            collective_id=0, has_side_effects=True, vmem_limit_bytes=48 * 1024 * 1024
        ),
        cost_estimate=pl.CostEstimate(
            flops=4 * taps * side * side * tiles * ch * 2 * ch,
            bytes_accessed=3 * side * side * tiles * LANES * 2,
            transcendentals=side * side * tiles * ch,
        ),
    )(act, bnd, conv_weight[0], idx)
    return jnp.transpose(grad, (2, 0, 1, 3))[None], wg[None]


def solution(mesh):
    spec = P("section", ("ens", "tile"), None, None, "chan")
    return jax.shard_map(
        functools.partial(body, mesh.shape["tile"], mesh.shape["section"]),
        mesh=mesh,
        in_specs=(spec, spec, P("section", None, None, "chan"), P(), P()),
        out_specs=(spec, P("section", "ens", "tile", "chan")),
        check_vma=False,
    )
```

```python
import functools

import jax
import jax.numpy as jnp
from jax import lax
from jax.experimental import pallas as pl
from jax.experimental.pallas import tpu as pltpu
from jax.sharding import PartitionSpec as P

MESH = pl.DeviceIdType.MESH
LANES = 128
F32 = jnp.float32
BF16 = jnp.bfloat16
WIRE = jnp.bfloat16


def flat(x):
    return x.reshape(-1, x.shape[-1])


def kernel(
    n_tile, n_section, normalizer,
    act_hbm, bnd_hbm, w_hbm, idx_ref,
    grad_ref, wg_ref,
    act_ref, bnd_ref, w_ref,
    peri_src, inner_src, ring, inner, third, pad, strips, wother, wfull, activ, deriv, totals, acc, wsend, wrecv,
    l_sem, x_send, x_recv, z_send, z_recv, w_sems, c_send, c_recv, h_send, h_recv, g_send, g_recv,
):
    ens, me, sec, chan = (lax.axis_index(a) for a in ("ens", "tile", "section", "chan"))
    side, _, tiles, ch = act_ref.shape
    full = side - 1
    half_tiles = n_tile // 2
    other = 1 - chan
    sibling = (ens, me, sec, other)
    target = (ens, me, lax.rem(sec + n_section - 1, n_section), chan)
    source = (ens, me, lax.rem(sec + 1, n_section), chan)
    lead = ch // 3
    n_chunk = inner.shape[0]

    def remote(src, dst, ss, rs, dev):
        return pltpu.make_async_remote_copy(
            src_ref=src, dst_ref=dst, send_sem=ss, recv_sem=rs, device_id=dev, device_id_type=MESH
        )

    loads = [
        pltpu.make_async_copy(src, dst, l_sem.at[n])
        for n, (src, dst) in enumerate(((bnd_hbm, bnd_ref), (w_hbm, w_ref), (act_hbm, act_ref)))
    ]
    for copy in loads:
        copy.start()
    barrier = pltpu.get_barrier_semaphore()
    for dev in (sibling, target, source):
        pl.semaphore_signal(barrier, inc=1, device_id=dev, device_id_type=MESH)
    for step in range(1, n_tile):
        for k in range(2):
            dev = (ens, lax.rem(me + step, n_tile), sec, k)
            pl.semaphore_signal(barrier, inc=1, device_id=dev, device_id_type=MESH)

    rows_i = lax.broadcasted_iota(jnp.int32, (ch, LANES), 0)
    cols_i = lax.broadcasted_iota(jnp.int32, (ch, LANES), 1)
    eye = (rows_i == cols_i).astype(BF16)
    picks = [
        ((cols_i >= ch) & (rows_i - b * lead == cols_i - ch)).astype(BF16) for b in range(3)
    ]
    wide_i = lax.broadcasted_iota(jnp.int32, (LANES, LANES), 0)
    wide_j = lax.broadcasted_iota(jnp.int32, (LANES, LANES), 1)
    moves = [
        ((wide_i >= ch) & (wide_j == wide_i - ch + b * lead)).astype(BF16) for b in range(3)
    ]

    def packed(groups, b):
        out = jnp.dot(groups[b], eye, preferred_element_type=F32) + jnp.dot(
            groups[3], picks[b], preferred_element_type=F32
        )
        return out.astype(BF16).reshape(-1, tiles, LANES)

    def untail(blocks):
        total = jnp.dot(blocks[0], moves[0], preferred_element_type=F32)
        for b in range(1, 3):
            total = total + jnp.dot(blocks[b], moves[b], preferred_element_type=F32)
        return total.astype(BF16).reshape(-1, tiles, LANES)

    def keep(x):
        lane = lax.broadcasted_iota(jnp.int32, x.shape, x.ndim - 1)
        return jnp.where(lane < ch, x.astype(F32), 0.0).astype(BF16)

    loads[0].wait()
    groups = [
        flat(bnd_ref[0, 0:full]),
        flat(bnd_ref[0:full, full]),
        flat(bnd_ref[full, 1 : full + 1]),
        flat(bnd_ref[1 : full + 1, 0]),
    ]
    sends_peri = []
    for b in range(3):
        peri_src[b] = packed(groups, b)
        if b == 0:
            pl.semaphore_wait(barrier, 3 + 2 * (n_tile - 1))
        copy = remote(peri_src.at[b], ring.at[me, b], x_send.at[b], x_recv.at[b], target)
        copy.start()
        sends_peri.append(copy)
    def ready(m):
        first = 1 + 4 * m
        groups = [flat(bnd_ref[first + g, 1:full]) for g in range(4)]
        for b in range(3):
            inner_src[m, b] = packed(groups, b)
        return remote(inner_src.at[m], inner.at[m], x_send.at[3 + m], x_recv.at[3 + m], target)

    sends_inner = [ready(0)]
    sends_inner[0].start()
    sends_z = []
    for b in range(3):
        sends_peri[b].wait()
        for step in range(1, n_tile):
            dev = (ens, lax.rem(me + step, n_tile), sec, chan)
            copy = remote(
                ring.at[me, b], ring.at[me, b], z_send.at[step - 1, b], z_recv.at[step - 1, b], dev
            )
            copy.start()
            sends_z.append(copy)
    for m in range(1, n_chunk):
        sends_inner.append(ready(m))
        sends_inner[m].start()
    loads[1].wait()
    mine_c = pl.multiple_of(chan * ch, 16)
    other_c = pl.multiple_of(other * ch, 16)
    send_w = remote(w_ref.at[:, pl.ds(other_c, ch), :], wother, w_sems.at[0], w_sems.at[1], sibling)
    send_w.start()

    blocks = [ring[me, b] for b in range(3)]
    pad[1, 1 : full + 1, :, 0:LANES] = keep(blocks[0])
    pad[1 : full + 1, full + 1, :, 0:LANES] = keep(blocks[1])
    pad[full + 1, 2 : full + 2, :, 0:LANES] = keep(blocks[2])
    pad[2 : full + 2, 1, :, 0:LANES] = untail([flat(x) for x in blocks])

    def to_sibling(rows, cols, ss, rs):
        return remote(
            pad.at[rows, cols, :, 0:LANES], pad.at[rows, cols, :, LANES : 2 * LANES], ss, rs, sibling
        )

    inside = pl.ds(1, side)
    sends_c = [
        to_sibling(pl.ds(first, 1), inside, c_send.at[n_chunk + n], c_recv.at[n_chunk + n])
        for n, first in enumerate((1, side))
    ]
    for copy in sends_c:
        copy.start()

    none = jnp.zeros((side, tiles, 2 * LANES), BF16)
    pad[0, 1 : side + 1] = none
    pad[side + 1, 1 : side + 1] = none
    pad[1 : side + 1, 0] = none
    pad[1 : side + 1, side + 1] = none
    acc[...] = jnp.zeros_like(acc)
    wfull[...] = jnp.zeros_like(wfull)
    wfull[:, :, 0:ch] = w_ref[:, pl.ds(mine_c, ch), :]
    send_w.wait()
    wfull[:, :, LANES : LANES + ch] = wother[...]

    loads[2].wait()

    def silu_row(i, carry):
        v = act_ref[i].astype(F32)
        logistic = 1.0 / (1.0 + jnp.exp(-v))
        activ[i] = (v * logistic).astype(BF16)
        deriv[i] = logistic * (1.0 + v * (1.0 - logistic))
        return carry

    lax.fori_loop(0, side, silu_row, 0)

    def times(view, q):
        return lax.dot_general(
            view, wfull[q], (((1,), (1,)), ((), ())), preferred_element_type=F32
        )

    def against(a, view):
        return lax.dot_general(a, view, (((0,), (0,)), ((), ())), preferred_element_type=F32)

    def row(i, carry):
        a = flat(activ[i])
        total = None
        for q, (di, dj) in enumerate(((0, 0), (-1, 0), (0, -1), (1, 0), (0, 1))):
            view = flat(pad[i + 1 - di, 1 - dj : 1 - dj + side])
            term = times(view, q)
            total = term if total is None else total + term
            acc[q] += against(a, view)
        total = total.reshape(side, tiles, ch)
        totals[i] = total
        grad_ref[i] = (deriv[i] * total).astype(BF16)
        return carry

    for m in range(n_chunk):
        sends_inner[m].wait()
        first = 2 + 4 * m
        blocks = [inner[m, b] for b in range(3)]
        for b in range(3):
            pad[first + b, 2 : full + 1, :, 0:LANES] = keep(blocks[b])
        pad[first + 3, 2 : full + 1, :, 0:LANES] = untail([flat(x) for x in blocks])
        copy = to_sibling(pl.ds(first, 4), inside, c_send.at[m], c_recv.at[m])
        copy.start()
        if m == 0:
            for early in sends_c:
                early.wait()
        copy.wait()
        lax.fori_loop(4 * m, 4 * m + 4 if m + 1 < n_chunk else side, row, 0)

    depth = wg_ref.shape[1]
    owner = chan * half_tiles

    def share(part, q0, q1):
        for j in range(half_tiles):
            for k in range(2):
                wsend[j, k, q0:q1] = acc[
                    q0:q1, j * depth : (j + 1) * depth, k * LANES : (k + 1) * LANES
                ].astype(wsend.dtype)
                copy = outgoing(part, q0, q1, j, k)
                if k == 0:

                    @pl.when(owner + j != me)
                    def _():
                        copy.start()

                    @pl.when(owner + j == me)
                    def _():
                        wrecv[me, q0:q1] = wsend[j, 0, q0:q1]
                else:
                    copy.start()

    def outgoing(part, q0, q1, j, k):
        there = (ens, owner + j, sec, chan if k == 0 else other)
        return remote(
            wsend.at[j, k, q0:q1], wrecv.at[me, q0:q1], g_send.at[part, j, k], g_recv.at[part, me], there
        )

    n_tap = acc.shape[0]
    parts = ((0, 1), (1, n_tap))
    share(0, *parts[0])

    for copy in sends_z:
        copy.wait()
    for z in range(n_tile):
        third[z] = untail([flat(ring[z, b]) for b in range(3)])

    def edge(s, p):
        if s == 0:
            part = ring[:, 0, p] if p < full else ring[:, 1, 0]
        elif s == 3:
            part = ring[:, 1, p] if p < full else ring[:, 2, full - 1]
        elif s == 2:
            part = third[:, full - 1] if p == 0 else ring[:, 2, p - 1]
        else:
            part = ring[:, 0, 0] if p == 0 else third[:, p - 1]
        return flat(part)

    n_all = n_tile * tiles
    which = idx_ref[...]
    spots = lax.broadcasted_iota(jnp.int32, (4 * tiles, 4 * n_all), 1)
    plain = (which == spots).astype(F32).astype(BF16)
    turned = (which == spots + 4 * n_all).astype(F32).astype(BF16)
    for p in range(side):
        ahead = jnp.concatenate([edge(s, p) for s in range(4)], axis=0)
        behind = jnp.concatenate([edge(s, full - p) for s in range(4)], axis=0)
        strip = jnp.dot(plain, ahead, preferred_element_type=F32) + jnp.dot(
            turned, behind, preferred_element_type=F32
        )
        strips[:, p, :, 0:LANES] = keep(strip).reshape(4, tiles, LANES)
    send_h = remote(
        strips.at[:, :, :, 0:LANES], strips.at[:, :, :, LANES : 2 * LANES], h_send.at[0], h_recv.at[0], sibling
    )
    send_h.start()
    send_h.wait()
    taps_of = (3, 4, 1, 2)
    for k, q in enumerate(taps_of):
        a = (activ[0], activ[:, 0], activ[full], activ[:, full])[k]
        acc[q] += against(flat(a), flat(strips[k]))
    share(1, *parts[1])
    for k, q in enumerate(taps_of):
        term = times(flat(strips[k]), q).reshape(side, tiles, ch)
        if k == 0:
            totals[0] += term
        elif k == 1:
            totals[:, 0] += term
        elif k == 2:
            totals[full] += term
        else:
            totals[:, full] += term
    grad_ref[0] = (deriv[0] * totals[0]).astype(BF16)
    grad_ref[full] = (deriv[full] * totals[full]).astype(BF16)
    grad_ref[1:full, 0] = (deriv[1:full, 0] * totals[1:full, 0]).astype(BF16)
    grad_ref[1:full, full] = (deriv[1:full, full] * totals[1:full, full]).astype(BF16)

    from_chan = me // half_tiles
    for part, (q0, q1) in enumerate(parts):
        for z in range(n_tile):

            @pl.when((me != z) | (from_chan != chan))
            def _():
                remote(
                    wsend.at[0, 0, q0:q1], wrecv.at[z, q0:q1], g_send.at[part, 0, 0], g_recv.at[part, z], sibling
                ).wait_recv()

    total = wrecv[0].astype(F32)
    for z in range(1, n_tile):
        total = total + wrecv[z].astype(F32)
    wg_ref[...] = total[:, :, 0:ch] * normalizer
    for part, (q0, q1) in enumerate(parts):
        for j in range(half_tiles):
            for k in range(2):
                copy = outgoing(part, q0, q1, j, k)
                if k == 0:

                    @pl.when(owner + j != me)
                    def _():
                        copy.wait_send()
                else:
                    copy.wait_send()


def body(n_tile, n_section, activation, boundary, conv_weight, neighbours, rotations):
    _, tiles, side, _, ch = activation.shape
    taps, c_all = conv_weight.shape[1:3]
    depth = c_all // n_tile
    n_all = n_tile * tiles
    act = jnp.transpose(activation[0], (1, 2, 0, 3))
    bnd = jnp.transpose(boundary[0], (1, 2, 0, 3))
    start = lax.axis_index("tile") * tiles
    near = lax.dynamic_slice_in_dim(neighbours.T, start, tiles, 1)
    turns = lax.dynamic_slice_in_dim(rotations.T, start, tiles, 1)
    src = (jnp.arange(4, dtype=jnp.int32)[:, None] + 2 - turns) % 4
    flipped = (turns == 2) | ((turns == 1) & (src % 2 == 0)) | ((turns == 3) & (src % 2 == 1))
    idx = (src * n_all + near + jnp.where(flipped, 4 * n_all, 0)).reshape(4 * tiles, 1)
    full = side - 1
    chunks = (side - 2) // 4
    vm = pl.BlockSpec(memory_space=pltpu.VMEM)
    normalizer = float(n_all * side * side) ** -0.5
    dma = pltpu.SemaphoreType.DMA
    grad, wg = pl.pallas_call(
        functools.partial(kernel, n_tile, n_section, normalizer),
        out_shape=(
            jax.ShapeDtypeStruct((side, side, tiles, ch), BF16),
            jax.ShapeDtypeStruct((taps, depth, ch), F32),
        ),
        in_specs=[pl.BlockSpec(memory_space=pltpu.HBM)] * 3 + [vm],
        out_specs=(vm, vm),
        scratch_shapes=[
            pltpu.VMEM((side, side, tiles, ch), BF16),
            pltpu.VMEM((side, side, tiles, ch), BF16),
            pltpu.VMEM((taps, c_all, ch), BF16),
            pltpu.VMEM((3, full, tiles, LANES), BF16),
            pltpu.VMEM((chunks, 3, side - 2, tiles, LANES), BF16),
            pltpu.VMEM((n_tile, 3, full, tiles, LANES), BF16),
            pltpu.VMEM((chunks, 3, side - 2, tiles, LANES), BF16),
            pltpu.VMEM((n_tile, full, tiles, LANES), BF16),
            pltpu.VMEM((side + 2, side + 2, tiles, 2 * LANES), BF16),
            pltpu.VMEM((4, side, tiles, 2 * LANES), BF16),
            pltpu.VMEM((taps, ch, ch), BF16),
            pltpu.VMEM((taps, ch, 2 * LANES), BF16),
            pltpu.VMEM((side, side, tiles, ch), BF16),
            pltpu.VMEM((side, side, tiles, ch), F32),
            pltpu.VMEM((side, side, tiles, ch), F32),
            pltpu.VMEM((taps, ch, 2 * LANES), F32),
            pltpu.VMEM((n_tile // 2, 2, taps, depth, LANES), WIRE),
            pltpu.VMEM((n_tile, taps, depth, LANES), WIRE),
            dma((3,)),
            dma((3 + chunks,)),
            dma((3 + chunks,)),
            dma((n_tile - 1, 3)),
            dma((n_tile - 1, 3)),
            dma((2,)),
            dma((chunks + 2,)),
            dma((chunks + 2,)),
            dma((1,)),
            dma((1,)),
            dma((2, n_tile // 2, 2)),
            dma((2, n_tile)),
        ],
        compiler_params=pltpu.CompilerParams(
            collective_id=0, has_side_effects=True, vmem_limit_bytes=60 * 1024 * 1024
        ),
        cost_estimate=pl.CostEstimate(
            flops=4 * taps * side * side * tiles * ch * 2 * ch,
            bytes_accessed=3 * side * side * tiles * LANES * 2,
            transcendentals=side * side * tiles * ch,
        ),
    )(act, bnd, conv_weight[0], idx)
    return jnp.transpose(grad, (2, 0, 1, 3))[None], wg[None]


def solution(mesh):
    spec = P("section", ("ens", "tile"), None, None, "chan")
    return jax.shard_map(
        functools.partial(body, mesh.shape["tile"], mesh.shape["section"]),
        mesh=mesh,
        in_specs=(spec, spec, P("section", None, None, "chan"), P(), P()),
        out_specs=(spec, P("section", "ens", "tile", "chan")),
        check_vma=False,
    )
```
